32 devices in a mesh: dp: 16 (over z, x, core), tensor: 2 (over y).
Axes of the slice: x: 2, y: 2, z: 4, core: 2. Of those that a mesh axis runs over, the one named last changes fastest.
Arguments:
- inputs: bfloat16 [4096, 1024], P(('dp', 'tensor')), may hold values from -6 to 6
- segment_ids: int32 [4096], P('dp'), may hold values from 0 to 4, as said below
- gain_in: float32 [1024], replicated, may hold values from 0.1 to 1.9
- w_query: bfloat16 [1024, 1024], P('dp', 'tensor'), may hold values from -0.1875 to 0.1875
- w_key: bfloat16 [1024, 1024], P('dp', 'tensor'), may hold values from -0.1875 to 0.1875
- w_value: bfloat16 [1024, 2048], P('dp', 'tensor'), may hold values from -0.1875 to 0.1875
- w_gate: bfloat16 [1024, 2048], P('dp', 'tensor'), may hold values from -0.1875 to 0.1875
- w_decay: bfloat16 [1024, 2, 8], P('dp', None, 'tensor'), may hold values from -0.1875 to 0.1875
- conv_query: float32 [4, 1024], replicated, may hold values from -3 to 3
- conv_key: float32 [4, 1024], replicated, may hold values from -3 to 3
- conv_value: float32 [4, 2048], replicated, may hold values from -3 to 3
- a_log: float32 [8], replicated, may hold values from 0 to 2.77
- dt_bias: float32 [8], replicated, may hold values from -6.9 to -2.3
- gain_mix: float32 [256], replicated, may hold values from 0.1 to 1.9
- w_out: bfloat16 [2048, 1024], P('tensor', 'dp'), may hold values from -0.125 to 0.125
- gain_ffn: float32 [1024], replicated, may hold values from 0.1 to 1.9
- w_ffn_gate: bfloat16 [1024, 2816], P('dp', 'tensor'), may hold values from -0.1875 to 0.1875
- w_ffn_up: bfloat16 [1024, 2816], P('dp', 'tensor'), may hold values from -0.1875 to 0.1875
- w_ffn_down: bfloat16 [2816, 1024], P('tensor', 'dp'), may hold values from -0.15625 to 0.15625
- out_grad: bfloat16 [4096, 1024], P(('dp', 'tensor')), may hold values from -6 to 6
Outputs:
- output: bfloat16 [4096, 1024], P(('dp', 'tensor'))
- grad_inputs: float32 [4096, 1024], P(('dp', 'tensor'))
- grad_gain_in: float32 [1024], replicated
- grad_w_query: float32 [1024, 1024], P('dp', 'tensor')
- grad_w_key: float32 [1024, 1024], P('dp', 'tensor')
- grad_w_value: float32 [1024, 2048], P('dp', 'tensor')
- grad_w_gate: float32 [1024, 2048], P('dp', 'tensor')
- grad_w_decay: float32 [1024, 2, 8], P('dp', None, 'tensor')
- grad_conv_query: float32 [4, 1024], replicated
- grad_conv_key: float32 [4, 1024], replicated
- grad_conv_value: float32 [4, 2048], replicated
- grad_a_log: float32 [8], replicated
- grad_dt_bias: float32 [8], replicated
- mixer_gain_gradient: float32 [256], replicated
- grad_w_out: float32 [2048, 1024], P('tensor', 'dp')
- grad_gain_ffn: float32 [1024], replicated
- grad_w_ffn_gate: float32 [1024, 2816], P('dp', 'tensor')
- grad_w_ffn_up: float32 [1024, 2816], P('dp', 'tensor')
- grad_w_ffn_down: float32 [2816, 1024], P('tensor', 'dp')
The draws below stay inside these ranges and needn't reach their ends.
Inputs may be any that keep to these rules, and one draw needn't show every extreme that they name: `segment_ids`: in each aligned block of 256 tokens the ids start at 0 and rise by one at each new segment, never falling; every block holds exactly 5 segments, and one of them covers tokens 256 // 4 to 192 of the block.
All inputs are finite; a program needn't handle non-finite values.
Results may differ from the reference program's by a relative error of at most 0.0131.
Values may be sent and summed in bfloat16 or wider, within the bound.
A program may use at most 192 MiB of HBM per device.

```python
import math
import jax
import jax.numpy as jnp
from jax import lax

D = 1024
H = 8
DK = 128
DV = 256
FF = 2816
CONV = 4
SPAN = 64
EDGE_DOCS = 2
TOK_GRP = 256
TOKENS = 4096


def draw_segment_ids(key, part):
    key = jax.random.fold_in(key, 11)
    quarter = TOK_GRP // 4
    blocks_total = TOKENS // TOK_GRP
    positions = jnp.arange(TOK_GRP, dtype=jnp.int32)

    def one_pack(pack_key):
        early_key, late_key = jax.random.split(pack_key)
        early_starts = jax.random.permutation(early_key, quarter - 1)[:EDGE_DOCS] + 1
        late_starts = jax.random.permutation(late_key, quarter - 1)[:EDGE_DOCS] + 3 * quarter + 1
        chosen = jnp.concatenate([early_starts, late_starts]).astype(jnp.int32)
        starts = jnp.sum((positions[:, None] == chosen[None, :]).astype(jnp.int32), axis=1)
        return jnp.cumsum(starts).astype(jnp.int32)
    return jax.vmap(one_pack)(jax.random.split(key, blocks_total)).reshape(TOKENS)


def levels(own_key, extent, shards, low, top_value):
    gain, own = 1.0, jax.random.fold_in(own_key, 6)
    for dim, blocks in shards:
        draws = jnp.exp(jax.random.uniform(jax.random.fold_in(own, dim), (blocks,), jnp.float32, low / len(shards), top_value / len(shards)))
        gain = gain * jnp.repeat(draws, extent[dim] // blocks).reshape([-1 if axis == dim else 1 for axis in range(len(extent))])
    return gain


def normal_values(key, shape, spread, bound, cuts=(), held_as=jnp.bfloat16):
    values = jax.random.normal(key, shape, jnp.float32) * spread
    if len(cuts) > 0:
        values = levels(key, shape, cuts, -0.22, 0.18) * values
    return jnp.clip(values, min=-bound, max=bound).astype(held_as)


def setup_inputs(seed: int = 0) -> dict:
    arg_keys = jax.random.split(jax.random.key(seed), 21)
    return {
        "inputs": normal_values(arg_keys[0], (TOKENS, D), 1.0, 6.0, ((0, 32),)),
        "segment_ids": draw_segment_ids(jax.random.fold_in(arg_keys[20], 71), 0),
        "gain_in": jnp.clip(1.0 + 0.18 * jax.random.normal(arg_keys[2], (D,), jnp.float32), 0.1, 1.9),
        "w_query": normal_values(arg_keys[3], (D, H * DK), D ** -0.5, 0.1875, ((0, 16), (1, 2))),
        "w_key": normal_values(arg_keys[4], (D, H * DK), D ** -0.5, 0.1875, ((0, 16), (1, 2))),
        "w_value": normal_values(arg_keys[5], (D, H * DV), D ** -0.5, 0.1875, ((0, 16), (1, 2))),
        "w_gate": normal_values(arg_keys[6], (D, H * DV), D ** -0.5, 0.1875, ((0, 16), (1, 2))),
        "w_decay": normal_values(arg_keys[7], (D, 2, H), D ** -0.5, 0.1875, ((0, 16), (2, 2))),
        "conv_query": normal_values(arg_keys[8], (CONV, H * DK), 0.5, 3.0, (), jnp.float32),
        "conv_key": normal_values(arg_keys[9], (CONV, H * DK), 0.5, 3.0, (), jnp.float32),
        "conv_value": normal_values(arg_keys[10], (CONV, H * DV), 0.5, 3.0, (), jnp.float32),
        "a_log": jnp.clip(jax.random.uniform(arg_keys[11], (H,), jnp.float32, 0.0, 2.77), 0.0, 2.77),
        "dt_bias": jnp.clip(jax.random.uniform(arg_keys[12], (H,), jnp.float32, -6.9, -2.3), -6.9, -2.3),
        "gain_mix": jnp.clip(1.0 + 0.18 * jax.random.normal(arg_keys[13], (DV,), jnp.float32), 0.1, 1.9),
        "w_out": normal_values(arg_keys[14], (H * DV, D), (H * DV) ** -0.5, 0.125, ((0, 2), (1, 16))),
        "gain_ffn": jnp.clip(1.0 + 0.18 * jax.random.normal(arg_keys[15], (D,), jnp.float32), 0.1, 1.9),
        "w_ffn_gate": normal_values(arg_keys[16], (D, FF), D ** -0.5, 0.1875, ((0, 16), (1, 2))),
        "w_ffn_up": normal_values(arg_keys[17], (D, FF), D ** -0.5, 0.1875, ((0, 16), (1, 2))),
        "w_ffn_down": normal_values(arg_keys[18], (FF, D), (FF // 2) ** -0.5, 0.15625, ((0, 2), (1, 16))),
        "out_grad": normal_values(arg_keys[19], (TOKENS, D), 1.0, 6.0, ((0, 32),)),
    }


@jax.custom_vjp
def low(v):
    return lax.optimization_barrier(v.astype(jnp.bfloat16)).astype(jnp.float32)

@jax.custom_vjp
def low_back(v):
    return v

def low_keep(v):
    return (low(v), None)

def low_pass(kept, grad):
    return (grad,)

def back_keep(v):
    return (v, None)

def back_low(kept, grad):
    return (low(grad),)
low.defvjp(low_keep, low_pass)
low_back.defvjp(back_keep, back_low)
highest = lax.Precision.HIGHEST
norm_epsilon = 1e-06

def rms_rows(matrix):
    return matrix * lax.rsqrt(lax.optimization_barrier(jnp.mean(matrix * matrix, axis=-1, keepdims=True)) + norm_epsilon)

def causal_conv(input_signal, kernel, segment_ids):
    length = input_signal.shape[0]
    widths = kernel.shape[0]
    summed = input_signal * kernel[widths - 1]
    for offset in range(1, widths):
        shifted = jnp.concatenate([jnp.zeros((offset, input_signal.shape[1]), jnp.float32), input_signal[:length - offset]], axis=0)
        shifted_ids = jnp.concatenate([jnp.full((offset,), -1, jnp.int32), segment_ids[:length - offset]])
        matches = (shifted_ids == segment_ids).astype(jnp.float32)
        summed = summed + shifted * kernel[widths - 1 - offset] * matches[:, None]
    return jax.nn.silu(summed)

def unit_heads(tensor3, factor):
    return tensor3 * lax.rsqrt(lax.optimization_barrier(jnp.sum(tensor3 * tensor3, axis=-1, keepdims=True)) + norm_epsilon) * factor

def segment_update(state_holder, segment_parts):
    running_state, closing_segment = state_holder
    span_query, span_keys, span_values, span_strength, span_decay, span_ids = segment_parts
    block_len = span_ids.shape[0]
    cumulative = jnp.cumsum(span_decay, axis=-1)
    row_index = lax.broadcasted_iota(jnp.int32, (block_len, block_len), 0)
    col_index = lax.broadcasted_iota(jnp.int32, (block_len, block_len), 1)
    same_seg = span_ids[:, None] == span_ids[None, :]
    lower_mask = jnp.logical_and(row_index >= col_index, same_seg).astype(jnp.float32)
    strict = jnp.logical_and(row_index > col_index, same_seg).astype(jnp.float32)
    difference = cumulative[:, :, None] - cumulative[:, None, :]
    within = jnp.exp(jnp.minimum(difference, 0.0))
    carried = (span_ids == closing_segment).astype(jnp.float32)
    entering = jnp.exp(cumulative) * carried[None, :]
    inner_kk = jnp.einsum('hid,hjd->hij', span_keys, span_keys, precision=highest)
    system = jnp.eye(block_len, dtype=jnp.float32)[None] + span_strength[:, :, None] * inner_kk * within * strict[None]
    from_state = jnp.einsum('hid,hde->hie', span_keys, running_state, precision=highest)
    target = span_strength[:, :, None] * (span_values - entering[:, :, None] * from_state)
    solved = lax.linalg.triangular_solve(system, target, left_side=True, lower=True, transpose_a=False, conjugate_a=False, unit_diagonal=True)
    inner_qk = jnp.einsum('hid,hjd->hij', span_query, span_keys, precision=highest)
    result = entering[:, :, None] * jnp.einsum('hid,hde->hie', span_query, running_state, precision=highest)
    result = result + jnp.einsum('hij,hje->hie', inner_qk * within * lower_mask[None], solved, precision=highest)
    tail_weight = within[:, block_len - 1, :] * lower_mask[block_len - 1][None, :]
    new_state = entering[:, block_len - 1][:, None, None] * running_state
    new_state = new_state + jnp.einsum('hjd,hje->hde', span_keys * tail_weight[:, :, None], solved, precision=highest)
    return ((new_state, span_ids[block_len - 1]), result)

def delta_rule(query_heads, key_heads, value_heads, strength, decay_log, segment_ids):
    head_count, length = strength.shape
    blocks_count = length // SPAN

    def cut_blocks(tensor):
        return jnp.moveaxis(tensor.reshape((head_count, blocks_count, SPAN) + tensor.shape[2:]), 1, 0)
    segment_parts = (cut_blocks(query_heads), cut_blocks(key_heads), cut_blocks(value_heads), cut_blocks(strength), cut_blocks(decay_log), segment_ids.reshape(blocks_count, SPAN))
    initial = (jnp.zeros((head_count, query_heads.shape[2], value_heads.shape[2]), jnp.float32), jnp.int32(-1))
    final_state, results = lax.scan(jax.checkpoint(segment_update), initial, segment_parts)
    return jnp.moveaxis(results, 0, 1).reshape(head_count, length, value_heads.shape[2])

def mixing_core(query_raw, key_raw, value_raw, gate_raw, decay_raw, segment_ids, conv_query, conv_key, conv_value, a_log, dt_bias, gain_mix):
    length = query_raw.shape[0]
    head_count = a_log.shape[0]
    head_dim = query_raw.shape[1] // head_count
    value_dim = gain_mix.shape[0]
    query_heads = unit_heads(causal_conv(query_raw, conv_query, segment_ids).reshape(length, head_count, head_dim), head_dim ** (-0.5))
    key_heads = unit_heads(causal_conv(key_raw, conv_key, segment_ids).reshape(length, head_count, head_dim), 1.0)
    value_heads = causal_conv(value_raw, conv_value, segment_ids).reshape(length, head_count, value_dim)
    strength = jax.nn.sigmoid(decay_raw[:, 1, :])
    decay_log = -jnp.exp(a_log) * jax.nn.softplus(decay_raw[:, 0, :] + dt_bias)
    mixed_heads = delta_rule(jnp.transpose(query_heads, (1, 0, 2)), jnp.transpose(key_heads, (1, 0, 2)), jnp.transpose(value_heads, (1, 0, 2)), strength.T, decay_log.T, segment_ids)
    mixed_heads = jnp.transpose(mixed_heads, (1, 0, 2))
    normed = mixed_heads * lax.rsqrt(lax.optimization_barrier(jnp.mean(mixed_heads * mixed_heads, axis=-1, keepdims=True)) + norm_epsilon) * gain_mix
    gated = normed * jax.nn.silu(gate_raw.reshape(length, head_count, value_dim))
    return gated.reshape(length, head_count * value_dim)

def layer_forward(pack_rows, pack_ids, weights):
    gain_in, w_query, w_key, w_value, w_gate, w_decay, conv_query, conv_key, conv_value, a_log, dt_bias, gain_mix, w_out, gain_ffn, w_ffn_gate, w_ffn_up, w_ffn_down = weights
    normed_in = low(rms_rows(pack_rows) * gain_in)

    def project(matrix):
        return jnp.dot(normed_in, matrix, precision=highest)
    query_raw = low_back(project(w_query))
    key_raw = low_back(project(w_key))
    value_raw = low_back(project(w_value))
    gate_raw = low_back(project(w_gate))
    decay_raw = low_back(project(w_decay.reshape(w_decay.shape[0], -1))).reshape(-1, 2, a_log.shape[0])
    mixed_gated = low(mixing_core(query_raw, key_raw, value_raw, gate_raw, decay_raw, pack_ids, conv_query, conv_key, conv_value, a_log, dt_bias, gain_mix))
    residual = pack_rows + low_back(jnp.dot(mixed_gated, w_out, precision=highest))
    normed_mid = low(rms_rows(residual) * gain_ffn)
    ffn_gate = low_back(jnp.dot(normed_mid, w_ffn_gate, precision=highest))
    ffn_up = low_back(jnp.dot(normed_mid, w_ffn_up, precision=highest))
    hidden = low(jax.nn.silu(ffn_gate) * ffn_up)
    return residual + jnp.dot(hidden, w_ffn_down, precision=highest)

def reference(inputs, segment_ids, gain_in, w_query, w_key, w_value, w_gate, w_decay, conv_query, conv_key, conv_value, a_log, dt_bias, gain_mix, w_out, gain_ffn, w_ffn_gate, w_ffn_up, w_ffn_down, out_grad):
    weights = tuple((weight_arg.astype(jnp.float32) for weight_arg in (gain_in, w_query, w_key, w_value, w_gate, w_decay, conv_query, conv_key, conv_value, a_log, dt_bias, gain_mix, w_out, gain_ffn, w_ffn_gate, w_ffn_up, w_ffn_down)))
    packs = TOKENS // TOK_GRP
    per_step = math.gcd(packs, max(1, 4096 // TOK_GRP))
    grouped_ids = segment_ids.reshape(packs // per_step, per_step, TOK_GRP)

    def forward(rows_all, weight_set):

        def one_group(group_pair):
            group_rows, group_ids = group_pair
            return jax.vmap(lambda pack_rows, pack_ids: layer_forward(pack_rows, pack_ids, weight_set))(group_rows, group_ids)
        shaped = rows_all.reshape(packs // per_step, per_step, TOK_GRP, D)
        return lax.map(jax.checkpoint(one_group), (shaped, grouped_ids)).reshape(TOKENS, D)
    output, pullback = jax.vjp(forward, inputs.astype(jnp.float32), weights)
    grad_inputs, weight_grads = pullback(out_grad.astype(jnp.float32))
    return (output.astype(jnp.bfloat16), grad_inputs, weight_grads[0], weight_grads[1], weight_grads[2], weight_grads[3], weight_grads[4], weight_grads[5], weight_grads[6], weight_grads[7], weight_grads[8], weight_grads[9], weight_grads[10], weight_grads[11], weight_grads[12], weight_grads[13], weight_grads[14], weight_grads[15], weight_grads[16])
```

```python
import functools

import jax
import jax.numpy as jnp
from jax import lax
from jax.experimental import pallas as pl
from jax.experimental.pallas import tpu as pltpu
from jax.sharding import PartitionSpec as P

norm_epsilon = 1e-06
LANES = 128
BASE = 8
f32 = jnp.float32
bf16 = jnp.bfloat16
NN = ((1,), (0,))
NT = ((1,), (1,))
TN = ((0,), (0,))


def rms_rows(matrix):
    return matrix * lax.rsqrt(jnp.mean(matrix * matrix, axis=-1, keepdims=True) + norm_epsilon)


def rms_back(matrix, incoming, gain):
    scale = lax.rsqrt(jnp.mean(matrix * matrix, axis=-1, keepdims=True) + norm_epsilon)
    normed = matrix * scale
    scaled = incoming * gain
    grad_matrix = scale * (scaled - normed * jnp.mean(scaled * normed, axis=-1, keepdims=True))
    return (grad_matrix, jnp.sum(incoming * normed, axis=0))


def dot(left, right, dims):
    return lax.dot_general(left, right, (dims, ((), ())), preferred_element_type=f32)


def contract_last(left, right):
    return dot(left, right, NT)


def contract_first(left, right):
    return dot(left, right, TN)


def split(value):
    high = value.astype(bf16)
    return (high, (value - high.astype(f32)).astype(bf16))


def mul(left, right, dims=NN):
    return dot(left[0], right[0], dims) + (
        dot(left[0], right[1], dims) + dot(left[1], right[0], dims)
    )


def mask_mul(mask, value, dims, mask_first=True):
    first = value.astype(bf16)
    rest = value - first.astype(f32)
    second = rest.astype(bf16)
    third = (rest - second.astype(f32)).astype(bf16)
    total = None
    for part in (third, second, first):
        term = dot(mask, part, dims) if mask_first else dot(part, mask, dims)
        total = term if total is None else total + term
    return total


def silu_back(value, sig):
    return sig * (1.0 + value * (1.0 - sig))


def tap_masks(ids_col):
    length = ids_col.shape[0]
    row = lax.broadcasted_iota(jnp.int32, (length, 1), 0)
    masks = [None]
    for offset in range(1, 4):
        shifted = pltpu.roll(jnp.broadcast_to(ids_col, (length, LANES)), offset, 0)[:, :1]
        masks.append(jnp.logical_and(row >= offset, shifted == ids_col).astype(f32))
    return masks


def conv_pre(signal, taps, masks):
    total = signal * taps[3:4]
    for offset in range(1, 4):
        total = total + pltpu.roll(signal, offset, 0) * taps[3 - offset : 4 - offset] * masks[offset]
    return total


def conv_back(signal, taps, masks, grad):
    length = signal.shape[0]
    grad_signal = grad * taps[3:4]
    rows = [jnp.sum(grad * signal, axis=0, keepdims=True)]
    for offset in range(1, 4):
        masked = grad * masks[offset]
        rows.append(jnp.sum(masked * pltpu.roll(signal, offset, 0), axis=0, keepdims=True))
        grad_signal = (
            grad_signal + pltpu.roll(masked, length - offset, 0) * taps[3 - offset : 4 - offset]
        )
    return (grad_signal, rows)


def unit(conv, factor):
    scale = lax.rsqrt(jnp.sum(conv * conv, axis=-1, keepdims=True) + norm_epsilon)
    return (conv * (scale * factor), scale)


def unit_back(conv, scale, factor, grad):
    inner = jnp.sum(grad * conv, axis=-1, keepdims=True) * scale * scale
    return (scale * factor) * (grad - conv * inner)


def pair_masks(ids_col, ids_row):
    length = ids_col.shape[0]
    row = lax.broadcasted_iota(jnp.int32, (length, length), 0)
    col = lax.broadcasted_iota(jnp.int32, (length, length), 1)
    same = ids_col == ids_row
    lower = jnp.logical_and(row >= col, same).astype(f32)
    strict = jnp.logical_and(row > col, same).astype(f32)
    return (row, col, lower, strict)


def decay_parts(block, a_row, dt_row, heads):
    lane = lax.broadcasted_iota(jnp.int32, block.shape, 1)
    shifted = block + dt_row
    soft = jnp.maximum(shifted, 0.0) + jnp.log1p(jnp.exp(-jnp.abs(shifted)))
    logs = jnp.where(lane < heads, -jnp.exp(a_row) * soft, 0.0)
    return (lane, shifted, logs)


def unit_lower_inverses(systems, row, col):
    length = row.shape[0]
    eye = (row == col).astype(f32)
    near = ((row // BASE) == (col // BASE)).astype(f32)
    blocks = [system * near for system in systems]
    parts = [split(block) for block in blocks]
    squares = [split(mul(part, part)) for part in parts]
    fourths = [split(mul(square, square)) for square in squares]
    inverses = [eye - block for block in blocks]
    inverses = [inv + mul(split(inv), square) for inv, square in zip(inverses, squares)]
    inverses = [inv + mul(split(inv), fourth) for inv, fourth in zip(inverses, fourths)]
    size = BASE
    while size < length:
        off = jnp.logical_and(
            (row // (2 * size)) == (col // (2 * size)), (row // size) != (col // size)
        ).astype(f32)
        held = [split(inv) for inv in inverses]
        steps = [split(mul(split(system * off), part)) for system, part in zip(systems, held)]
        inverses = [inv - mul(part, step) for inv, part, step in zip(inverses, held, steps)]
        size *= 2
    return inverses


def core_common(dims, proj, ids_col, ids_row, taps_q, taps_k, taps_v, a_row, dt_row):
    heads, key_dim, value_dim = dims
    keys, values = (heads * key_dim, heads * value_dim)
    masks = tap_masks(ids_col)
    row, col, lower, strict = pair_masks(ids_col, ids_row)
    tail = proj[:, 2 * keys + 2 * values :]
    lane, shifted, logs = decay_parts(tail, a_row, dt_row, heads)
    gates = jax.nn.sigmoid(tail)
    low_mask = lower.astype(bf16)
    cum = mask_mul(low_mask, logs, NN)
    cum_turned = mask_mul(low_mask, logs, ((0,), (1,)), mask_first=False)
    pre_q = conv_pre(proj[:, :keys], taps_q, masks)
    pre_k = conv_pre(proj[:, keys : 2 * keys], taps_k, masks)
    pre_v = conv_pre(proj[:, 2 * keys : 2 * keys + values], taps_v, masks)
    per_head = []
    for head in range(heads):
        span = slice(head * key_dim, (head + 1) * key_dim)
        wide = slice(head * value_dim, (head + 1) * value_dim)
        pq, pk, pv = (pre_q[:, span], pre_k[:, span], pre_v[:, wide])
        sq, sk, sv = (jax.nn.sigmoid(pq), jax.nn.sigmoid(pk), jax.nn.sigmoid(pv))
        cq, ck, value = (pq * sq, pk * sk, pv * sv)
        query, scale_q = unit(cq, key_dim ** (-0.5))
        keyvec, scale_k = unit(ck, 1.0)
        query_s, key_s = (split(query), split(keyvec))
        strength = gates[:, heads + head : heads + head + 1]
        within = jnp.exp(
            jnp.minimum(cum[:, head : head + 1] - cum_turned[head : head + 1, :], 0.0)
        )
        per_head.append(
            dict(
                pq=pq, pk=pk, pv=pv, sq=sq, sk=sk, sv=sv, cq=cq, ck=ck, value=value,
                scale_q=scale_q, scale_k=scale_k, query_s=query_s, key_s=key_s,
                strength=strength, w_low=within * lower, w_strict=within * strict,
                kk=mul(key_s, key_s, NT), qk=mul(query_s, key_s, NT),
                gate=proj[:, 2 * keys + values + head * value_dim :][:, :value_dim],
            )
        )
    return (per_head, masks, row, col, lane, shifted, logs, gates, low_mask)


def core_forward(
    dims, proj, ids_col, ids_row, taps_q, taps_k, taps_v, a_row, dt_row, gain, gated, inverse
):
    heads, _, value_dim = dims
    per_head, _, row, col, *_ = core_common(
        dims, proj[...], ids_col[...], ids_row[...], taps_q[...], taps_k[...], taps_v[...],
        a_row[...], dt_row[...],
    )
    inverses = unit_lower_inverses(
        [item["strength"] * item["kk"] * item["w_strict"] for item in per_head], row, col
    )
    for head, item in enumerate(per_head):
        inverse[head] = inverses[head]
        solved = mul(split(inverses[head]), split(item["strength"] * item["value"]))
        mixed = mul(split(item["qk"] * item["w_low"]), split(solved))
        scale = lax.rsqrt(jnp.mean(mixed * mixed, axis=-1, keepdims=True) + norm_epsilon)
        gate = item["gate"]
        gated[:, head * value_dim : (head + 1) * value_dim] = (
            mixed * scale * gain[...] * (gate * jax.nn.sigmoid(gate))
        ).astype(bf16)


def core_backward(
    dims, proj, ids_col, ids_row, taps_q, taps_k, taps_v, a_row, dt_row, gain, inverse, grad_out,
    grad_proj, grad_q, grad_k, grad_v, grad_small,
):
    heads, key_dim, value_dim = dims
    keys, values = (heads * key_dim, heads * value_dim)
    raw = proj[...]
    tq, tk, tv, gains = (taps_q[...], taps_k[...], taps_v[...], gain[...])
    per_head, masks, row, col, lane, shifted, logs, gates, low_mask = core_common(
        dims, raw, ids_col[...], ids_row[...], tq, tk, tv, a_row[...], dt_row[...]
    )
    grad_cum = jnp.zeros(logs.shape, f32)
    grad_gates = jnp.zeros(logs.shape, f32)
    grad_gain = jnp.zeros(gains.shape, f32)
    for head, item in enumerate(per_head):
        span = slice(head * key_dim, (head + 1) * key_dim)
        wide = slice(head * value_dim, (head + 1) * value_dim)
        strength, value, gate = (item["strength"], item["value"], item["gate"])
        turned = split(inverse[head])
        solved = mul(turned, split(strength * value))
        solved_s = split(solved)
        attend = item["qk"] * item["w_low"]
        attend_s = split(attend)
        mixed = mul(attend_s, solved_s)
        scale = lax.rsqrt(jnp.mean(mixed * mixed, axis=-1, keepdims=True) + norm_epsilon)
        normed = mixed * scale
        sig = jax.nn.sigmoid(gate)
        incoming = grad_out[:, wide]
        through = incoming * (gate * sig)
        grad_gate = incoming * normed * gains * silu_back(gate, sig)
        grad_gain = grad_gain + jnp.sum(through * normed, axis=0, keepdims=True)
        scaled = through * gains
        grad_mixed = scale * (
            scaled - normed * jnp.mean(scaled * normed, axis=-1, keepdims=True)
        )
        grad_s = split(grad_mixed)
        grad_attend = mul(grad_s, solved_s, NT)
        grad_target = mul(turned, split(mul(attend_s, grad_s, TN)), TN)
        grad_system = -mul(split(grad_target), solved_s, NT) * item["w_strict"]
        weighted = grad_system * item["kk"]
        energy = grad_attend * attend + strength * weighted
        cum_grad = jnp.sum(energy - jnp.transpose(energy), axis=1, keepdims=True)
        strength_grad = jnp.sum(weighted, axis=1, keepdims=True) + jnp.sum(
            grad_target * value, axis=1, keepdims=True
        )
        grad_cum = jnp.where(lane == head, cum_grad, grad_cum)
        grad_gates = jnp.where(lane == heads + head, strength_grad, grad_gates)
        grad_qk = split(grad_attend * item["w_low"])
        grad_kk = grad_system * strength
        grad_kk = split(grad_kk + jnp.transpose(grad_kk))
        query_grad = mul(grad_qk, item["key_s"])
        key_grad = mul(grad_qk, item["query_s"], TN) + mul(grad_kk, item["key_s"])
        back_q = unit_back(item["cq"], item["scale_q"], key_dim ** (-0.5), query_grad)
        back_k = unit_back(item["ck"], item["scale_k"], 1.0, key_grad)
        back_q = back_q * silu_back(item["pq"], item["sq"])
        back_k = back_k * silu_back(item["pk"], item["sk"])
        back_v = strength * grad_target * silu_back(item["pv"], item["sv"])
        for start, width, taps, where, back, out in (
            (0, span, tq, head * key_dim, back_q, grad_q),
            (keys, span, tk, head * key_dim, back_k, grad_k),
            (2 * keys, wide, tv, head * value_dim, back_v, grad_v),
        ):
            size = back.shape[1]
            signal = raw[:, start + where : start + where + size]
            low_grad, tap_rows = conv_back(signal, taps[:, width], masks, back)
            grad_proj[:, start + where : start + where + size] = low_grad.astype(bf16)
            for offset in range(4):
                out[3 - offset : 4 - offset, width] = tap_rows[offset]
        place = 2 * keys + values + head * value_dim
        grad_proj[:, place : place + value_dim] = grad_gate.astype(bf16)
    grad_logs = mask_mul(low_mask, grad_cum, TN)
    grad_shift = grad_logs * -jnp.exp(a_row[...]) * jax.nn.sigmoid(shifted)
    grad_shift = jnp.where(lane < heads, grad_shift, 0.0)
    tail = grad_shift + grad_gates * gates * (1.0 - gates)
    grad_proj[:, 2 * keys + 2 * values :] = tail.astype(bf16)
    grad_small[...] = jnp.zeros(grad_small.shape, f32)
    grad_small[0:1, :] = grad_gain
    grad_small[1:2, :LANES] = jnp.sum(grad_logs * logs, axis=0, keepdims=True)
    grad_small[2:3, :LANES] = jnp.sum(grad_shift, axis=0, keepdims=True)


def core_params():
    return pltpu.CompilerParams(vmem_limit_bytes=56 * 1024 * 1024)


def call_forward(dims, length, operands):
    heads, _, value_dim = dims
    return pl.pallas_call(
        functools.partial(core_forward, dims),
        out_shape=(
            jax.ShapeDtypeStruct((length, heads * value_dim), bf16),
            jax.ShapeDtypeStruct((heads, length, length), f32),
        ),
        compiler_params=core_params(),
        cost_estimate=pl.CostEstimate(
            flops=120 * heads * length**3, bytes_accessed=6 * 1024 * 1024, transcendentals=1000000
        ),
        name="core_forward",
    )(*operands)


def call_backward(dims, length, operands):
    heads, key_dim, value_dim = dims
    keys, values = (heads * key_dim, heads * value_dim)
    return pl.pallas_call(
        functools.partial(core_backward, dims),
        out_shape=(
            jax.ShapeDtypeStruct((length, 2 * keys + 2 * values + LANES), bf16),
            jax.ShapeDtypeStruct((4, keys), f32),
            jax.ShapeDtypeStruct((4, keys), f32),
            jax.ShapeDtypeStruct((4, values), f32),
            jax.ShapeDtypeStruct((8, value_dim), f32),
        ),
        compiler_params=core_params(),
        cost_estimate=pl.CostEstimate(
            flops=120 * heads * length**3, bytes_accessed=8 * 1024 * 1024, transcendentals=1000000
        ),
        name="core_backward",
    )(*operands)


def swap(value):
    return lax.ppermute(value, "tensor", [(0, 1), (1, 0)])


def both_halves(own, rank):
    other = swap(own)
    first = jnp.where(rank == 0, own, other)
    second = jnp.where(rank == 0, other, own)
    return jnp.concatenate([first, second], axis=0)


def sum_halves(terms, rank):
    rows = terms.shape[0] // 2
    sent = lax.dynamic_slice_in_dim(terms, (1 - rank) * rows, rows, 0).astype(bf16)
    kept = lax.dynamic_slice_in_dim(terms, rank * rows, rows, 0)
    return kept + swap(sent).astype(f32)


def sum_everywhere(value, groups):
    value = value + swap(value)
    step = 1
    while step < groups:
        value = value + lax.ppermute(value, "dp", [(i, i ^ step) for i in range(groups)])
        step *= 2
    return value


def per_device(
    groups,
    inputs,
    segment_ids,
    gain_in,
    w_query,
    w_key,
    w_value,
    w_gate,
    w_decay,
    conv_query,
    conv_key,
    conv_value,
    a_log,
    dt_bias,
    gain_mix,
    w_out,
    gain_ffn,
    w_ffn_gate,
    w_ffn_up,
    w_ffn_down,
    out_grad,
):
    rank = lax.axis_index("tensor")
    heads = w_decay.shape[2]
    keys = w_query.shape[1]
    values = w_value.shape[1]
    hidden_units = w_ffn_gate.shape[1]
    rows_held = w_query.shape[0]
    dims = (heads, keys // heads, values // heads)
    length = segment_ids.shape[0]

    mixer_held = jnp.concatenate(
        [
            w_query, w_key, w_value, w_gate, w_decay.reshape(rows_held, 2 * heads),
            jnp.zeros((rows_held, LANES - 2 * heads), bf16),
        ],
        axis=1,
    )
    full_mixer = lax.all_gather(mixer_held, "dp", axis=0, tiled=True)
    block_held = jnp.concatenate([w_out.T, w_ffn_gate, w_ffn_up, w_ffn_down.T], axis=1)
    full_block = lax.all_gather(block_held, "dp", axis=0, tiled=True)
    out_turned = full_block[:, :values]
    full_pair = full_block[:, values : values + 2 * hidden_units]
    down_turned = full_block[:, values + 2 * hidden_units :]

    inputs_wide = inputs.astype(f32)
    normed_in = both_halves((rms_rows(inputs_wide) * gain_in).astype(bf16), rank)
    grad_rows_out = both_halves(out_grad, rank)

    def part(whole, width, along):
        return lax.dynamic_slice_in_dim(whole, rank * width, width, along)

    def lane_row(vector):
        return jnp.pad(part(vector, heads, 0), (0, LANES - heads)).reshape(1, LANES)

    proj = jnp.dot(normed_in, full_mixer, preferred_element_type=f32)
    operands = (
        proj, segment_ids.reshape(length, 1), segment_ids.reshape(1, length),
        part(conv_query, keys, 1), part(conv_key, keys, 1), part(conv_value, values, 1),
        lane_row(a_log), lane_row(dt_bias), gain_mix.reshape(1, -1),
    )
    mixed_gated, inverse = call_forward(dims, length, operands)
    residual = inputs_wide + sum_halves(contract_last(mixed_gated, out_turned), rank)
    normed_mid = both_halves((rms_rows(residual) * gain_ffn).astype(bf16), rank)
    ffn_pair = jnp.dot(normed_mid, full_pair, preferred_element_type=f32)
    ffn_gate, ffn_up = (ffn_pair[:, :hidden_units], ffn_pair[:, hidden_units:])
    sigmoid_gate = jax.nn.sigmoid(ffn_gate)
    hidden = (ffn_gate * sigmoid_gate * ffn_up).astype(bf16)
    output = (residual + sum_halves(contract_last(hidden, down_turned), rank)).astype(bf16)
    grad_hidden = jnp.dot(grad_rows_out, down_turned, preferred_element_type=f32)
    grad_pair = jnp.concatenate(
        [
            (grad_hidden * ffn_up * silu_back(ffn_gate, sigmoid_gate)).astype(bf16),
            (grad_hidden * (ffn_gate * sigmoid_gate)).astype(bf16),
        ],
        axis=1,
    )
    grad_mid = sum_halves(contract_last(grad_pair, full_pair), rank)
    grad_mid_rows, grad_gain_ffn = rms_back(residual, grad_mid, gain_ffn)
    grad_resid = out_grad.astype(f32) + grad_mid_rows
    grad_rows_mid = both_halves(grad_resid.astype(bf16), rank)
    block_grads = jnp.concatenate(
        [
            contract_first(grad_rows_mid, mixed_gated).astype(bf16),
            contract_first(normed_mid, grad_pair).astype(bf16),
            contract_first(grad_rows_out, hidden).astype(bf16),
        ],
        axis=1,
    )
    block_shard = lax.psum_scatter(block_grads, "dp", scatter_dimension=0, tiled=True).astype(f32)
    grad_mixed = jnp.dot(grad_rows_mid, out_turned, preferred_element_type=f32)
    grad_proj, grad_conv_q, grad_conv_k, grad_conv_v, grad_small = call_backward(
        dims, length, operands + (inverse, grad_mixed)
    )
    mixer_grads = contract_first(normed_in, grad_proj).astype(bf16)
    mixer_shard = lax.psum_scatter(mixer_grads, "dp", scatter_dimension=0, tiled=True).astype(f32)
    grad_in = sum_halves(contract_last(grad_proj, full_mixer), rank)
    grad_in_rows, grad_gain_in = rms_back(inputs_wide, grad_in, gain_in)
    grad_inputs = grad_resid + grad_in_rows

    def place_part(part_grad, whole):
        along = whole.ndim - 1
        return lax.dynamic_update_slice_in_dim(
            jnp.zeros(whole.shape, f32), part_grad, rank * part_grad.shape[along], along
        )

    small_parts = (
        grad_gain_in,
        place_part(grad_conv_q, conv_query),
        place_part(grad_conv_k, conv_key),
        place_part(grad_conv_v, conv_value),
        place_part(grad_small[1, :heads], a_log),
        place_part(grad_small[2, :heads], dt_bias),
        grad_small[0],
        grad_gain_ffn,
    )
    flat = jnp.concatenate([item.reshape(-1) for item in small_parts])
    padding = -flat.shape[0] % (8 * LANES)
    flat = sum_everywhere(jnp.pad(flat, (0, padding)).reshape(-1, LANES), groups).reshape(-1)
    small, at = ([], 0)
    for item in small_parts:
        small.append(flat[at : at + item.size].reshape(item.shape))
        at += item.size
    at_up, at_down = (values + hidden_units, values + 2 * hidden_units)
    at_decay = 2 * keys + 2 * values
    return (
        output,
        grad_inputs,
        small[0],
        mixer_shard[:, :keys],
        mixer_shard[:, keys : 2 * keys],
        mixer_shard[:, 2 * keys : 2 * keys + values],
        mixer_shard[:, 2 * keys + values : at_decay],
        mixer_shard[:, at_decay : at_decay + 2 * heads].reshape(rows_held, 2, heads),
        small[1],
        small[2],
        small[3],
        small[4],
        small[5],
        small[6],
        block_shard[:, :values].T,
        small[7],
        block_shard[:, values:at_up],
        block_shard[:, at_up:at_down],
        block_shard[:, at_down:].T,
    )


def solution(mesh):
    placed = (
        P(("dp", "tensor"), None),
        P("dp"),
        P(),
        P("dp", "tensor"),
        P("dp", "tensor"),
        P("dp", "tensor"),
        P("dp", "tensor"),
        P("dp", None, "tensor"),
        P(),
        P(),
        P(),
        P(),
        P(),
        P(),
        P("tensor", "dp"),
        P(),
        P("dp", "tensor"),
        P("dp", "tensor"),
        P("tensor", "dp"),
        P(("dp", "tensor"), None),
    )
    return jax.shard_map(
        functools.partial(per_device, mesh.shape["dp"]),
        mesh=mesh,
        in_specs=placed,
        out_specs=(
            P(("dp", "tensor"), None),
            P(("dp", "tensor"), None),
            P(),
            P("dp", "tensor"),
            P("dp", "tensor"),
            P("dp", "tensor"),
            P("dp", "tensor"),
            P("dp", None, "tensor"),
            P(),
            P(),
            P(),
            P(),
            P(),
            P(),
            P("tensor", "dp"),
            P(),
            P("dp", "tensor"),
            P("dp", "tensor"),
            P("tensor", "dp"),
        ),
        check_vma=False,
    )
```

```python
import functools

import jax
import jax.numpy as jnp
from jax import lax
from jax.experimental import pallas as pl
from jax.experimental.pallas import tpu as pltpu
from jax.sharding import PartitionSpec as P

norm_epsilon = 1e-06
LANES = 128
BASE = 8
f32 = jnp.float32
bf16 = jnp.bfloat16
NN = ((1,), (0,))
NT = ((1,), (1,))
TN = ((0,), (0,))


def rms_rows(matrix):
    return matrix * lax.rsqrt(jnp.mean(matrix * matrix, axis=-1, keepdims=True) + norm_epsilon)


def rms_back(matrix, incoming, gain):
    scale = lax.rsqrt(jnp.mean(matrix * matrix, axis=-1, keepdims=True) + norm_epsilon)
    normed = matrix * scale
    scaled = incoming * gain
    grad_matrix = scale * (scaled - normed * jnp.mean(scaled * normed, axis=-1, keepdims=True))
    return (grad_matrix, jnp.sum(incoming * normed, axis=0))


def dot(left, right, dims):
    return lax.dot_general(left, right, (dims, ((), ())), preferred_element_type=f32)


def contract_last(left, right):
    return dot(left, right, NT)


def contract_first(left, right):
    return dot(left, right, TN)


def split(value):
    high = value.astype(bf16)
    return (high, (value - high.astype(f32)).astype(bf16))


def mul(left, right, dims=NN):
    return dot(left[0], right[0], dims) + (
        dot(left[0], right[1], dims) + dot(left[1], right[0], dims)
    )


def mask_mul(mask, value, dims, mask_first=True):
    first = value.astype(bf16)
    rest = value - first.astype(f32)
    second = rest.astype(bf16)
    third = (rest - second.astype(f32)).astype(bf16)
    total = None
    for part in (third, second, first):
        term = dot(mask, part, dims) if mask_first else dot(part, mask, dims)
        total = term if total is None else total + term
    return total


def silu_back(value, sig):
    return sig * (1.0 + value * (1.0 - sig))


def tap_masks(ids_col):
    length = ids_col.shape[0]
    row = lax.broadcasted_iota(jnp.int32, (length, 1), 0)
    masks = [None]
    for offset in range(1, 4):
        shifted = pltpu.roll(jnp.broadcast_to(ids_col, (length, LANES)), offset, 0)[:, :1]
        masks.append(jnp.logical_and(row >= offset, shifted == ids_col).astype(f32))
    return masks


def conv_pre(signal, taps, masks):
    total = signal * taps[3:4]
    for offset in range(1, 4):
        total = total + pltpu.roll(signal, offset, 0) * taps[3 - offset : 4 - offset] * masks[offset]
    return total


def conv_back(signal, taps, masks, grad):
    length = signal.shape[0]
    grad_signal = grad * taps[3:4]
    rows = [jnp.sum(grad * signal, axis=0, keepdims=True)]
    for offset in range(1, 4):
        masked = grad * masks[offset]
        rows.append(jnp.sum(masked * pltpu.roll(signal, offset, 0), axis=0, keepdims=True))
        grad_signal = (
            grad_signal + pltpu.roll(masked, length - offset, 0) * taps[3 - offset : 4 - offset]
        )
    return (grad_signal, rows)


def unit(conv, factor):
    scale = lax.rsqrt(jnp.sum(conv * conv, axis=-1, keepdims=True) + norm_epsilon)
    return (conv * (scale * factor), scale)


def unit_back(conv, scale, factor, grad):
    inner = jnp.sum(grad * conv, axis=-1, keepdims=True) * scale * scale
    return (scale * factor) * (grad - conv * inner)


def pair_masks(ids_col, ids_row):
    length = ids_col.shape[0]
    row = lax.broadcasted_iota(jnp.int32, (length, length), 0)
    col = lax.broadcasted_iota(jnp.int32, (length, length), 1)
    same = ids_col == ids_row
    lower = jnp.logical_and(row >= col, same).astype(f32)
    strict = jnp.logical_and(row > col, same).astype(f32)
    return (row, col, lower, strict)


def decay_parts(block, a_row, dt_row, heads):
    lane = lax.broadcasted_iota(jnp.int32, block.shape, 1)
    shifted = block + dt_row
    soft = jnp.maximum(shifted, 0.0) + jnp.log1p(jnp.exp(-jnp.abs(shifted)))
    logs = jnp.where(lane < heads, -jnp.exp(a_row) * soft, 0.0)
    return (lane, shifted, logs)


def unit_lower_inverses(systems, row, col):
    length = row.shape[0]
    eye = (row == col).astype(f32)
    near = ((row // BASE) == (col // BASE)).astype(f32)
    blocks = [system * near for system in systems]
    parts = [split(block) for block in blocks]
    squares = [split(mul(part, part)) for part in parts]
    fourths = [split(mul(square, square)) for square in squares]
    inverses = [eye - block for block in blocks]
    inverses = [inv + mul(split(inv), square) for inv, square in zip(inverses, squares)]
    inverses = [inv + mul(split(inv), fourth) for inv, fourth in zip(inverses, fourths)]
    size = BASE
    while size < length:
        off = jnp.logical_and(
            (row // (2 * size)) == (col // (2 * size)), (row // size) != (col // size)
        ).astype(f32)
        held = [split(inv) for inv in inverses]
        steps = [split(mul(split(system * off), part)) for system, part in zip(systems, held)]
        inverses = [inv - mul(part, step) for inv, part, step in zip(inverses, held, steps)]
        size *= 2
    return inverses


def core_common(dims, proj, ids_col, ids_row, taps_q, taps_k, taps_v, a_row, dt_row):
    heads, key_dim, value_dim = dims
    keys, values = (heads * key_dim, heads * value_dim)
    masks = tap_masks(ids_col)
    row, col, lower, strict = pair_masks(ids_col, ids_row)
    tail = proj[:, 2 * keys + 2 * values :]
    lane, shifted, logs = decay_parts(tail, a_row, dt_row, heads)
    gates = jax.nn.sigmoid(tail)
    low_mask = lower.astype(bf16)
    cum = mask_mul(low_mask, logs, NN)
    cum_turned = mask_mul(low_mask, logs, ((0,), (1,)), mask_first=False)
    pre_q = conv_pre(proj[:, :keys], taps_q, masks)
    pre_k = conv_pre(proj[:, keys : 2 * keys], taps_k, masks)
    pre_v = conv_pre(proj[:, 2 * keys : 2 * keys + values], taps_v, masks)
    per_head = []
    for head in range(heads):
        span = slice(head * key_dim, (head + 1) * key_dim)
        wide = slice(head * value_dim, (head + 1) * value_dim)
        pq, pk, pv = (pre_q[:, span], pre_k[:, span], pre_v[:, wide])
        sq, sk, sv = (jax.nn.sigmoid(pq), jax.nn.sigmoid(pk), jax.nn.sigmoid(pv))
        cq, ck, value = (pq * sq, pk * sk, pv * sv)
        query, scale_q = unit(cq, key_dim ** (-0.5))
        keyvec, scale_k = unit(ck, 1.0)
        query_s, key_s = (split(query), split(keyvec))
        strength = gates[:, heads + head : heads + head + 1]
        within = jnp.exp(
            jnp.minimum(cum[:, head : head + 1] - cum_turned[head : head + 1, :], 0.0)
        )
        per_head.append(
            dict(
                pq=pq, pk=pk, pv=pv, sq=sq, sk=sk, sv=sv, cq=cq, ck=ck, value=value,
                scale_q=scale_q, scale_k=scale_k, query_s=query_s, key_s=key_s,
                strength=strength, w_low=within * lower, w_strict=within * strict,
                kk=mul(key_s, key_s, NT), qk=mul(query_s, key_s, NT),
                gate=proj[:, 2 * keys + values + head * value_dim :][:, :value_dim],
            )
        )
    return (per_head, masks, row, col, lane, shifted, logs, gates, low_mask)


def core_forward(
    dims, proj, ids_col, ids_row, taps_q, taps_k, taps_v, a_row, dt_row, gain, gated, inverse
):
    heads, _, value_dim = dims
    per_head, _, row, col, *_ = core_common(
        dims, proj[...], ids_col[...], ids_row[...], taps_q[...], taps_k[...], taps_v[...],
        a_row[...], dt_row[...],
    )
    inverses = unit_lower_inverses(
        [item["strength"] * item["kk"] * item["w_strict"] for item in per_head], row, col
    )
    for head, item in enumerate(per_head):
        inverse[head] = inverses[head]
        solved = mul(split(inverses[head]), split(item["strength"] * item["value"]))
        mixed = mul(split(item["qk"] * item["w_low"]), split(solved))
        scale = lax.rsqrt(jnp.mean(mixed * mixed, axis=-1, keepdims=True) + norm_epsilon)
        gate = item["gate"]
        gated[:, head * value_dim : (head + 1) * value_dim] = (
            mixed * scale * gain[...] * (gate * jax.nn.sigmoid(gate))
        ).astype(bf16)


def core_backward(
    dims, proj, ids_col, ids_row, taps_q, taps_k, taps_v, a_row, dt_row, gain, inverse, grad_out,
    grad_proj, grad_q, grad_k, grad_v, grad_small,
):
    heads, key_dim, value_dim = dims
    keys, values = (heads * key_dim, heads * value_dim)
    raw = proj[...]
    tq, tk, tv, gains = (taps_q[...], taps_k[...], taps_v[...], gain[...])
    per_head, masks, row, col, lane, shifted, logs, gates, low_mask = core_common(
        dims, raw, ids_col[...], ids_row[...], tq, tk, tv, a_row[...], dt_row[...]
    )
    grad_cum = jnp.zeros(logs.shape, f32)
    grad_gates = jnp.zeros(logs.shape, f32)
    grad_gain = jnp.zeros(gains.shape, f32)
    for head, item in enumerate(per_head):
        span = slice(head * key_dim, (head + 1) * key_dim)
        wide = slice(head * value_dim, (head + 1) * value_dim)
        strength, value, gate = (item["strength"], item["value"], item["gate"])
        turned = split(inverse[head])
        solved = mul(turned, split(strength * value))
        solved_s = split(solved)
        attend = item["qk"] * item["w_low"]
        attend_s = split(attend)
        mixed = mul(attend_s, solved_s)
        scale = lax.rsqrt(jnp.mean(mixed * mixed, axis=-1, keepdims=True) + norm_epsilon)
        normed = mixed * scale
        sig = jax.nn.sigmoid(gate)
        incoming = grad_out[:, wide]
        through = incoming * (gate * sig)
        grad_gate = incoming * normed * gains * silu_back(gate, sig)
        grad_gain = grad_gain + jnp.sum(through * normed, axis=0, keepdims=True)
        scaled = through * gains
        grad_mixed = scale * (
            scaled - normed * jnp.mean(scaled * normed, axis=-1, keepdims=True)
        )
        grad_s = split(grad_mixed)
        grad_attend = mul(grad_s, solved_s, NT)
        grad_target = mul(turned, split(mul(attend_s, grad_s, TN)), TN)
        grad_system = -mul(split(grad_target), solved_s, NT) * item["w_strict"]
        weighted = grad_system * item["kk"]
        energy = grad_attend * attend + strength * weighted
        cum_grad = jnp.sum(energy - jnp.transpose(energy), axis=1, keepdims=True)
        strength_grad = jnp.sum(weighted, axis=1, keepdims=True) + jnp.sum(
            grad_target * value, axis=1, keepdims=True
        )
        grad_cum = jnp.where(lane == head, cum_grad, grad_cum)
        grad_gates = jnp.where(lane == heads + head, strength_grad, grad_gates)
        grad_qk = split(grad_attend * item["w_low"])
        grad_kk = grad_system * strength
        grad_kk = split(grad_kk + jnp.transpose(grad_kk))
        query_grad = mul(grad_qk, item["key_s"])
        key_grad = mul(grad_qk, item["query_s"], TN) + mul(grad_kk, item["key_s"])
        back_q = unit_back(item["cq"], item["scale_q"], key_dim ** (-0.5), query_grad)
        back_k = unit_back(item["ck"], item["scale_k"], 1.0, key_grad)
        back_q = back_q * silu_back(item["pq"], item["sq"])
        back_k = back_k * silu_back(item["pk"], item["sk"])
        back_v = strength * grad_target * silu_back(item["pv"], item["sv"])
        for start, width, taps, where, back, out in (
            (0, span, tq, head * key_dim, back_q, grad_q),
            (keys, span, tk, head * key_dim, back_k, grad_k),
            (2 * keys, wide, tv, head * value_dim, back_v, grad_v),
        ):
            size = back.shape[1]
            signal = raw[:, start + where : start + where + size]
            low_grad, tap_rows = conv_back(signal, taps[:, width], masks, back)
            grad_proj[:, start + where : start + where + size] = low_grad.astype(bf16)
            for offset in range(4):
                out[3 - offset : 4 - offset, width] = tap_rows[offset]
        place = 2 * keys + values + head * value_dim
        grad_proj[:, place : place + value_dim] = grad_gate.astype(bf16)
    grad_logs = mask_mul(low_mask, grad_cum, TN)
    grad_shift = grad_logs * -jnp.exp(a_row[...]) * jax.nn.sigmoid(shifted)
    grad_shift = jnp.where(lane < heads, grad_shift, 0.0)
    tail = grad_shift + grad_gates * gates * (1.0 - gates)
    grad_proj[:, 2 * keys + 2 * values :] = tail.astype(bf16)
    grad_small[...] = jnp.zeros(grad_small.shape, f32)
    grad_small[0:1, :] = grad_gain
    grad_small[1:2, :LANES] = jnp.sum(grad_logs * logs, axis=0, keepdims=True)
    grad_small[2:3, :LANES] = jnp.sum(grad_shift, axis=0, keepdims=True)


def core_params():
    return pltpu.CompilerParams(vmem_limit_bytes=56 * 1024 * 1024)


def call_forward(dims, length, operands):
    heads, _, value_dim = dims
    return pl.pallas_call(
        functools.partial(core_forward, dims),
        out_shape=(
            jax.ShapeDtypeStruct((length, heads * value_dim), bf16),
            jax.ShapeDtypeStruct((heads, length, length), f32),
        ),
        compiler_params=core_params(),
        cost_estimate=pl.CostEstimate(
            flops=120 * heads * length**3, bytes_accessed=6 * 1024 * 1024, transcendentals=1000000
        ),
        name="core_forward",
    )(*operands)


def call_backward(dims, length, operands):
    heads, key_dim, value_dim = dims
    keys, values = (heads * key_dim, heads * value_dim)
    return pl.pallas_call(
        functools.partial(core_backward, dims),
        out_shape=(
            jax.ShapeDtypeStruct((length, 2 * keys + 2 * values + LANES), bf16),
            jax.ShapeDtypeStruct((4, keys), f32),
            jax.ShapeDtypeStruct((4, keys), f32),
            jax.ShapeDtypeStruct((4, values), f32),
            jax.ShapeDtypeStruct((8, value_dim), f32),
        ),
        compiler_params=core_params(),
        cost_estimate=pl.CostEstimate(
            flops=120 * heads * length**3, bytes_accessed=8 * 1024 * 1024, transcendentals=1000000
        ),
        name="core_backward",
    )(*operands)


def swap(value):
    return lax.ppermute(value, "tensor", [(0, 1), (1, 0)])


def both_halves(own, rank):
    other = swap(own)
    first = jnp.where(rank == 0, own, other)
    second = jnp.where(rank == 0, other, own)
    return jnp.concatenate([first, second], axis=0)


def sum_halves(terms, rank):
    rows = terms.shape[0] // 2
    sent = lax.dynamic_slice_in_dim(terms, (1 - rank) * rows, rows, 0).astype(bf16)
    kept = lax.dynamic_slice_in_dim(terms, rank * rows, rows, 0)
    return kept + swap(sent).astype(f32)


def sum_everywhere(value, groups):
    value = value + swap(value)
    step = 1
    while step < groups:
        value = value + lax.ppermute(value, "dp", [(i, i ^ step) for i in range(groups)])
        step *= 2
    return value


def stage_bits(groups, odd):
    bits = [1 << place for place in range(groups.bit_length() - 1)]
    if odd and len(bits) > 2:
        bits[1], bits[2] = (bits[2], bits[1])
    return bits


def row_order(me, groups, width):
    rows = width // groups
    col = lax.broadcasted_iota(jnp.int32, (1, width), 1)
    place, inner = (col // rows, col % rows)
    flips = []
    for odd in (0, 1):
        flip = jnp.zeros_like(place)
        for depth, bit in enumerate(stage_bits(groups, odd)):
            flip = flip + ((place // (groups >> (depth + 1))) % 2) * bit
        flips.append(flip)
    flip = jnp.where((me + place // (width // rows // 2)) % 2 == 0, flips[0], flips[1])
    source = jnp.bitwise_xor(me, flip) * rows + inner
    return (lax.broadcasted_iota(jnp.int32, (width, width), 0) == source).astype(bf16)


def scatter_stages(ordered, groups, first, last):
    both = (stage_bits(groups, 0), stage_bits(groups, 1))
    for depth in range(first, min(last, len(both[0]))):
        half = ordered.shape[0] // 2
        pairs = [(i, i ^ both[i % 2][depth]) for i in range(groups)]
        arrived = lax.ppermute(ordered[half:], "dp", pairs)
        ordered = ordered[:half].astype(f32) + arrived.astype(f32)
        if depth + 1 < len(both[0]):
            ordered = ordered.astype(bf16)
    return ordered


def per_device(
    groups,
    inputs,
    segment_ids,
    gain_in,
    w_query,
    w_key,
    w_value,
    w_gate,
    w_decay,
    conv_query,
    conv_key,
    conv_value,
    a_log,
    dt_bias,
    gain_mix,
    w_out,
    gain_ffn,
    w_ffn_gate,
    w_ffn_up,
    w_ffn_down,
    out_grad,
):
    rank = lax.axis_index("tensor")
    heads = w_decay.shape[2]
    keys = w_query.shape[1]
    values = w_value.shape[1]
    hidden_units = w_ffn_gate.shape[1]
    rows_held = w_query.shape[0]
    dims = (heads, keys // heads, values // heads)
    length = segment_ids.shape[0]

    mixer_held = jnp.concatenate(
        [
            w_query, w_key, w_value, w_gate, w_decay.reshape(rows_held, 2 * heads),
            jnp.zeros((rows_held, LANES - 2 * heads), bf16),
            w_out.T, w_ffn_gate, w_ffn_up, w_ffn_down.T,
        ],
        axis=1,
    )
    full_held = lax.all_gather(mixer_held, "dp", axis=0, tiled=True)
    mixer_width = 2 * keys + 2 * values + LANES
    full_mixer, full_block = (full_held[:, :mixer_width], full_held[:, mixer_width:])
    order = row_order(lax.axis_index("dp"), groups, inputs.shape[1])

    def ordered_grads(rows, grads):
        turned = jnp.dot(rows, order, preferred_element_type=f32).astype(bf16)
        return contract_first(turned, grads).astype(bf16)

    out_turned = full_block[:, :values]
    full_pair = full_block[:, values : values + 2 * hidden_units]
    down_turned = full_block[:, values + 2 * hidden_units :]

    inputs_wide = inputs.astype(f32)
    normed_in = both_halves((rms_rows(inputs_wide) * gain_in).astype(bf16), rank)
    grad_rows_out = both_halves(out_grad, rank)

    def part(whole, width, along):
        return lax.dynamic_slice_in_dim(whole, rank * width, width, along)

    def lane_row(vector):
        return jnp.pad(part(vector, heads, 0), (0, LANES - heads)).reshape(1, LANES)

    proj = jnp.dot(normed_in, full_mixer, preferred_element_type=f32)
    operands = (
        proj, segment_ids.reshape(length, 1), segment_ids.reshape(1, length),
        part(conv_query, keys, 1), part(conv_key, keys, 1), part(conv_value, values, 1),
        lane_row(a_log), lane_row(dt_bias), gain_mix.reshape(1, -1),
    )
    mixed_gated, inverse = call_forward(dims, length, operands)
    residual = inputs_wide + sum_halves(contract_last(mixed_gated, out_turned), rank)
    normed_mid = both_halves((rms_rows(residual) * gain_ffn).astype(bf16), rank)
    ffn_pair = jnp.dot(normed_mid, full_pair, preferred_element_type=f32)
    ffn_gate, ffn_up = (ffn_pair[:, :hidden_units], ffn_pair[:, hidden_units:])
    sigmoid_gate = jax.nn.sigmoid(ffn_gate)
    hidden = (ffn_gate * sigmoid_gate * ffn_up).astype(bf16)
    output = (residual + sum_halves(contract_last(hidden, down_turned), rank)).astype(bf16)
    grad_hidden = jnp.dot(grad_rows_out, down_turned, preferred_element_type=f32)
    grad_pair = jnp.concatenate(
        [
            (grad_hidden * ffn_up * silu_back(ffn_gate, sigmoid_gate)).astype(bf16),
            (grad_hidden * (ffn_gate * sigmoid_gate)).astype(bf16),
        ],
        axis=1,
    )
    grad_mid = sum_halves(contract_last(grad_pair, full_pair), rank)
    grad_mid_rows, grad_gain_ffn = rms_back(residual, grad_mid, gain_ffn)
    grad_resid = out_grad.astype(f32) + grad_mid_rows
    grad_rows_mid = both_halves(grad_resid.astype(bf16), rank)
    stages = groups.bit_length()
    down_sum = scatter_stages(ordered_grads(grad_rows_out, hidden), groups, 0, 2)
    pair_sum = scatter_stages(ordered_grads(normed_mid, grad_pair), groups, 0, 1)
    out_sum = ordered_grads(grad_rows_mid, mixed_gated)
    grad_mixed = jnp.dot(grad_rows_mid, out_turned, preferred_element_type=f32)
    grad_mixed, down_sum, pair_sum, out_sum = lax.optimization_barrier(
        (grad_mixed, down_sum, pair_sum, out_sum)
    )
    down_sum = scatter_stages(down_sum, groups, 2, 3)
    pair_sum = scatter_stages(pair_sum, groups, 1, 2)
    out_sum = scatter_stages(out_sum, groups, 0, 1)
    grad_proj, grad_conv_q, grad_conv_k, grad_conv_v, grad_small = call_backward(
        dims, length, operands + (inverse, grad_mixed)
    )
    grad_proj, down_sum, pair_sum, out_sum = lax.optimization_barrier(
        (grad_proj, down_sum, pair_sum, out_sum)
    )
    mixer_shard = scatter_stages(ordered_grads(normed_in, grad_proj), groups, 0, stages)
    down_shard = scatter_stages(down_sum, groups, 3, stages)
    pair_shard = scatter_stages(pair_sum, groups, 2, stages)
    out_shard = scatter_stages(out_sum, groups, 1, stages)
    grad_in = sum_halves(contract_last(grad_proj, full_mixer), rank)
    grad_in_rows, grad_gain_in = rms_back(inputs_wide, grad_in, gain_in)
    grad_inputs = grad_resid + grad_in_rows

    def place_part(part_grad, whole):
        along = whole.ndim - 1
        return lax.dynamic_update_slice_in_dim(
            jnp.zeros(whole.shape, f32), part_grad, rank * part_grad.shape[along], along
        )

    small_parts = (
        grad_gain_in,
        place_part(grad_conv_q, conv_query),
        place_part(grad_conv_k, conv_key),
        place_part(grad_conv_v, conv_value),
        place_part(grad_small[1, :heads], a_log),
        place_part(grad_small[2, :heads], dt_bias),
        grad_small[0],
        grad_gain_ffn,
    )
    flat = jnp.concatenate([item.reshape(-1) for item in small_parts])
    padding = -flat.shape[0] % (8 * LANES)
    flat = sum_everywhere(jnp.pad(flat, (0, padding)).reshape(-1, LANES), groups).reshape(-1)
    small, at = ([], 0)
    for item in small_parts:
        small.append(flat[at : at + item.size].reshape(item.shape))
        at += item.size
    at_decay = 2 * keys + 2 * values
    return (
        output,
        grad_inputs,
        small[0],
        mixer_shard[:, :keys],
        mixer_shard[:, keys : 2 * keys],
        mixer_shard[:, 2 * keys : 2 * keys + values],
        mixer_shard[:, 2 * keys + values : at_decay],
        mixer_shard[:, at_decay : at_decay + 2 * heads].reshape(rows_held, 2, heads),
        small[1],
        small[2],
        small[3],
        small[4],
        small[5],
        small[6],
        out_shard.T,
        small[7],
        pair_shard[:, :hidden_units],
        pair_shard[:, hidden_units:],
        down_shard.T,
    )


def solution(mesh):
    placed = (
        P(("dp", "tensor"), None),
        P("dp"),
        P(),
        P("dp", "tensor"),
        P("dp", "tensor"),
        P("dp", "tensor"),
        P("dp", "tensor"),
        P("dp", None, "tensor"),
        P(),
        P(),
        P(),
        P(),
        P(),
        P(),
        P("tensor", "dp"),
        P(),
        P("dp", "tensor"),
        P("dp", "tensor"),
        P("tensor", "dp"),
        P(("dp", "tensor"), None),
    )
    return jax.shard_map(
        functools.partial(per_device, mesh.shape["dp"]),
        mesh=mesh,
        in_specs=placed,
        out_specs=(
            P(("dp", "tensor"), None),
            P(("dp", "tensor"), None),
            P(),
            P("dp", "tensor"),
            P("dp", "tensor"),
            P("dp", "tensor"),
            P("dp", "tensor"),
            P("dp", None, "tensor"),
            P(),
            P(),
            P(),
            P(),
            P(),
            P(),
            P("tensor", "dp"),
            P(),
            P("dp", "tensor"),
            P("dp", "tensor"),
            P("tensor", "dp"),
        ),
        check_vma=False,
    )
```
